32 devices in a mesh: stack: 8 (over y, x, core), rows: 4 (over z).
Axes of the slice: x: 2, y: 2, z: 4, core: 2. Of those that a mesh axis runs over, the one named last changes fastest.
Arguments:
- field: float32 [2, 32, 64, 1536], P(None, 'stack', 'rows'), may hold values from -6 to 6
- hess_xx: float32 [32, 64, 1536], P('stack', 'rows'), may hold values from 0.3 to 1.5
- hess_yy: float32 [32, 64, 1536], P('stack', 'rows'), may hold values from 0.3 to 1.5
- hess_xy: float32 [32, 64, 1536], P('stack', 'rows'), may hold values from -1 to 1
- gradient: float32 [2, 32, 64, 1536], P(None, 'stack', 'rows'), may hold values from -5.5 to 5.5
Outputs:
- updated: float32 [2, 32, 64, 1536], P(None, 'stack', 'rows')
The draws below stay inside these ranges and needn't reach their ends.
All inputs are finite; a program needn't handle non-finite values.
Results may differ from the reference program's by a relative error of at most 0.00002.
Values sent between devices are 32-bit elements; how exact they have to be, the bound alone decides.
A program may use at most 64 MiB of HBM per device.

```python
import math
import jax
import jax.numpy as jnp

WIDTH = 1536
SWEEPS = 6
SECTIONS = 32
HEIGHT = 64


def smooth_ripple(key):
    phases = jax.random.uniform(key, (3,), jnp.float32, 0.0, 2.0 * math.pi)
    section_pos = jnp.arange(SECTIONS).astype(jnp.float32) / SECTIONS
    row_pos = jnp.arange(HEIGHT).astype(jnp.float32) / HEIGHT
    column_pos = jnp.arange(WIDTH).astype(jnp.float32) / WIDTH
    along_sections = jnp.sin(2.0 * math.pi * section_pos + phases[0])[:, None, None]
    along_rows = jnp.sin(2.0 * math.pi * row_pos + phases[1])[None, :, None]
    along_columns = jnp.sin(2.0 * math.pi * column_pos + phases[2])[None, None, :]
    return (along_sections + along_rows + along_columns) / 3.0


def draw_field(key, part):
    key = jax.random.fold_in(key, 11)
    extent = (SECTIONS, HEIGHT, WIDTH)
    components = []
    for component in range(2):
        subkey = jax.random.fold_in(key, component)
        ripple = smooth_ripple(jax.random.fold_in(subkey, 1))
        factor = jnp.exp(jax.random.uniform(jax.random.fold_in(subkey, 2), extent, jnp.float32, math.log(0.65), math.log(1.3)))
        plateau = 4.3 + 0.3 * ripple
        components.append(plateau * factor)
    return jnp.stack(components).astype(jnp.float32)


def draw_gradient(key, part):
    key = jax.random.fold_in(key, 23)
    extent = (SECTIONS, HEIGHT, WIDTH)
    components = []
    for component in range(2):
        subkey = jax.random.fold_in(key, component)
        ripple = smooth_ripple(jax.random.fold_in(subkey, 1))
        factor = jnp.exp(jax.random.uniform(jax.random.fold_in(subkey, 2), extent, jnp.float32, math.log(0.65), math.log(1.3)))
        plateau = 3.8 + 0.3 * ripple
        components.append(plateau * factor)
    return jnp.stack(components).astype(jnp.float32)


def levels(stream_key, dims, cuts, least, top_value):
    gain, own = 1.0, jax.random.fold_in(stream_key, 6)
    for dim, blocks in cuts:
        steps = jnp.exp(jax.random.uniform(jax.random.fold_in(own, dim), (blocks,), jnp.float32, least / len(cuts), top_value / len(cuts)))
        gain = gain * jnp.repeat(steps, dims[dim] // blocks).reshape([-1 if axis == dim else 1 for axis in range(len(dims))])
    return gain


def setup_inputs(seed: int = 0) -> dict:
    key_of = jax.random.split(jax.random.key(seed), 6)
    field = draw_field(jax.random.fold_in(key_of[5], 71), 0)
    hess_xx = jnp.clip(jnp.exp(math.log(1.5) - 1.60943787 * jax.random.uniform(key_of[1], (SECTIONS, HEIGHT, WIDTH), jnp.float32) ** levels(key_of[1], (SECTIONS, HEIGHT, WIDTH), ((0, 8), (1, 4)), -0.2, 0.2)), 0.3, 1.5)
    hess_yy = jnp.clip(jnp.exp(math.log(1.5) - 1.60943787 * jax.random.uniform(key_of[2], (SECTIONS, HEIGHT, WIDTH), jnp.float32) ** levels(key_of[2], (SECTIONS, HEIGHT, WIDTH), ((0, 8), (1, 4)), -0.2, 0.2)), 0.3, 1.5)
    hess_xy = jnp.clip(jax.random.uniform(key_of[3], (SECTIONS, HEIGHT, WIDTH), jnp.float32, -1.0, 1.0) * levels(key_of[3], (SECTIONS, HEIGHT, WIDTH), ((0, 8), (1, 4)), -0.4, 0.0), -1.0, 1.0)
    gradient = draw_gradient(jax.random.fold_in(key_of[5], 71), 0)
    return {"field": field, "hess_xx": hess_xx, "hess_yy": hess_yy, "hess_xy": hess_xy, "gradient": gradient}


near_weight = 1.0
far_weight = 0.5
plane_weight = 1.0
diag_shift = 7.0


def sweep(field, hess_xx, hess_yy, hess_xy, gradient):
    stacked = jnp.pad(field, ((0, 0), (2, 2), (0, 0), (0, 0)))
    planar = jnp.pad(field, ((0, 0), (0, 0), (1, 1), (1, 1)))
    near = stacked[:, 1:-3] + stacked[:, 3:-1]
    far = stacked[:, :-4] + stacked[:, 4:]
    plane = planar[:, :, :-2, 1:-1] + planar[:, :, 2:, 1:-1] + planar[:, :, 1:-1, :-2] + planar[:, :, 1:-1, 2:]
    right = -gradient + near_weight * near + far_weight * far + plane_weight * plane
    diag_a = hess_xx + diag_shift
    diag_c = hess_yy + diag_shift
    determ = diag_a * diag_c - hess_xy * hess_xy
    new_x = (diag_c * right[0] - hess_xy * right[1]) / determ
    new_y = (diag_a * right[1] - hess_xy * right[0]) / determ
    return jnp.stack([new_x, new_y])


def reference(field, hess_xx, hess_yy, hess_xy, gradient):
    current = field
    for step in range(SWEEPS):
        current = sweep(current, hess_xx, hess_yy, hess_xy, gradient)
    return current
```

```python
import functools

import jax
import jax.numpy as jnp
from jax import lax
from jax.experimental import pallas as pl
from jax.experimental.pallas import tpu as pltpu
from jax.sharding import PartitionSpec as P

SWEEPS = 6
NEAR, FAR, PLANE, SHIFT = 1.0, 0.5, 1.0, 7.0
PAD = 128
CHUNKS = 4
AHEAD = 2


def kernel(n_stack, n_rows, detour, field, hxx, hyy, hxy, grad, out,
           u, g, ca, cc, cb, row_out, row_in, passing,
           load_sem, send_sem, recv_sem, pass_send, pass_in, pass_out, pass_recv, out_sem):
    sections, height, width = hxx.shape
    cw = width // CHUNKS
    half = height // 2
    s = lax.axis_index("stack")
    z = lax.axis_index("rows")
    has_left, has_right = s > 0, s < n_stack - 1
    has_up, has_down = z > 0, z < n_rows - 1
    left, right = (s - 1, z), (s + 1, z)
    up, down = (s, z - 1), (s, z + 1)
    sides = ((has_left, left), (has_right, right), (has_up, up), (has_down, down))

    lo, hi = n_stack // 2 - 1, n_stack // 2
    is_lo, is_hi, is_first, is_last = s == lo, s == hi, s == 0, s == n_stack - 1
    via_last, via_first = (n_stack - 1, z), (0, z)

    barrier = pltpu.get_barrier_semaphore()
    expected = jnp.int32(0)
    for exists, where in sides:
        expected = expected + exists.astype(jnp.int32)

        @pl.when(exists)
        def _():
            pl.semaphore_signal(barrier, inc=1, device_id=where)
    if detour:
        for who, peers in ((is_lo, (0, n_stack - 1)), (is_hi, (0, n_stack - 1)),
                           (is_first, (lo, hi)), (is_last, (lo, hi))):
            expected = expected + 2 * who.astype(jnp.int32)

            @pl.when(who)
            def _():
                for peer in peers:
                    pl.semaphore_signal(barrier, inc=1, device_id=(peer, z))

    loads = [
        pltpu.make_async_copy(field, u.at[0, :, 2:sections + 2, :, PAD:PAD + width], load_sem.at[0]),
        pltpu.make_async_copy(hxx, ca, load_sem.at[1]),
        pltpu.make_async_copy(hyy, cc, load_sem.at[2]),
        pltpu.make_async_copy(hxy, cb, load_sem.at[3]),
        pltpu.make_async_copy(grad, g, load_sem.at[4]),
    ]
    for load in loads:
        load.start()
    pl.semaphore_wait(barrier, expected)

    def cols(c):
        return pl.ds(pl.multiple_of(c * cw + PAD, 128), cw)

    def raw_cols(c):
        return pl.ds(pl.multiple_of(c * cw, 128), cw)

    def section_copy(t, c, d, rows, first=False):
        dst = u.at[t, :, 0:2, rows, cols(c)] if d == 0 else u.at[t, :, sections + 2:sections + 4, rows, cols(c)]
        if first:
            src = field.at[:, sections - 2:sections, rows, raw_cols(c)] if d == 0 else field.at[:, 0:2, rows, raw_cols(c)]
        else:
            src = u.at[t, :, sections:sections + 2, rows, cols(c)] if d == 0 else u.at[t, :, 2:4, rows, cols(c)]
        return pltpu.make_async_remote_copy(
            src_ref=src, dst_ref=dst, send_sem=send_sem.at[t, c, d], recv_sem=recv_sem.at[t, c, d],
            device_id=right if d == 0 else left)

    def pass_copy(t, c, d, first=False):
        rows = slice(half, height)
        if first:
            src = field.at[:, sections - 2:sections, rows, raw_cols(c)] if d == 0 else field.at[:, 0:2, rows, raw_cols(c)]
        else:
            src = u.at[t, :, sections:sections + 2, rows, cols(c)] if d == 0 else u.at[t, :, 2:4, rows, cols(c)]
        return pltpu.make_async_remote_copy(
            src_ref=src, dst_ref=passing.at[t, :, :, :, raw_cols(c)], send_sem=pass_send.at[t, c],
            recv_sem=pass_in.at[t, c], device_id=via_last if d == 0 else via_first)

    def onward_copy(t, c, d):
        rows = slice(half, height)
        dst = u.at[t, :, 0:2, rows, cols(c)] if d == 0 else u.at[t, :, sections + 2:sections + 4, rows, cols(c)]
        return pltpu.make_async_remote_copy(
            src_ref=passing.at[t, :, :, :, raw_cols(c)], dst_ref=dst, send_sem=pass_out.at[t, c],
            recv_sem=pass_recv.at[t, c], device_id=(hi if d == 0 else lo, z))

    def row_copy(t, c, d):
        return pltpu.make_async_remote_copy(
            src_ref=row_out.at[t, d, :, raw_cols(c)], dst_ref=row_in.at[t, d, :, raw_cols(c)],
            send_sem=send_sem.at[t, c, 2 + d], recv_sem=recv_sem.at[t, c, 2 + d],
            device_id=down if d == 0 else up)

    def each_section_copy(t, c, do, first=False):
        every, upper = slice(0, height), slice(0, half)
        for d, exists, split in ((0, has_right, is_lo), (1, has_left, is_hi)):
            if detour:
                @pl.when(split)
                def _():
                    do(section_copy(t, c, d, upper, first), pass_copy(t, c, d, first))

                @pl.when(exists & jnp.logical_not(split))
                def _():
                    do(section_copy(t, c, d, every, first), None)
            else:
                @pl.when(exists)
                def _():
                    do(section_copy(t, c, d, every, first), None)

    def start(copy, other):
        if other is not None:
            other.start()
        copy.start()

    def finish(copy, other):
        copy.wait_send()
        if other is not None:
            other.wait_send()

    def await_sections(t, c):
        every, upper = slice(0, height), slice(0, half)
        for d, exists, split in ((0, has_left, is_hi), (1, has_right, is_lo)):
            if detour:
                @pl.when(split)
                def _():
                    section_copy(t, c, d, upper).wait_recv()
                    onward_copy(t, c, d).wait_recv()

                @pl.when(exists & jnp.logical_not(split))
                def _():
                    section_copy(t, c, d, every).wait_recv()
            else:
                @pl.when(exists)
                def _():
                    section_copy(t, c, d, every).wait_recv()

    def send_rows(t, c):
        for d, exists, edge in ((0, has_down, height - 1), (1, has_up, 0)):
            for i in range(2):
                for k in range(sections):
                    at = i * sections + k
                    row_out[t, d, at:at + 1, raw_cols(c)] = u[t, i, 2 + k, edge:edge + 1, cols(c)]

            @pl.when(exists)
            def _():
                row_copy(t, c, d).start()

    def pass_on(j):
        t, c = lax.div(j, CHUNKS), lax.rem(j, CHUNKS)
        for d, who in ((0, is_last), (1, is_first)):
            @pl.when(who)
            def _():
                pass_copy(t, c, d).wait_recv()
                onward_copy(t, c, d).start()

    def over(count, body):
        lax.fori_loop(0, count, lambda i, _: (body(i), None)[1], None)

    over(CHUNKS, lambda c: each_section_copy(0, c, start, True))

    for t in range(SWEEPS):
        for at in (0, PAD + width):
            u[t, :, 2:sections + 2, :, at:at + PAD] = jnp.zeros((2, sections, height, PAD), jnp.float32)
    def zero(t):
        for exists, at in ((has_left, 0), (has_right, sections + 2)):
            @pl.when(jnp.logical_not(exists))
            def _():
                u[t, :, at:at + 2, :, PAD:PAD + width] = jnp.zeros((2, 2, height, width), jnp.float32)
        for d, exists in ((0, has_up), (1, has_down)):
            @pl.when(jnp.logical_not(exists))
            def _():
                row_in[t, d] = jnp.zeros((2 * sections, width), jnp.float32)
    over(SWEEPS, zero)

    loads[0].wait()
    over(CHUNKS, lambda c: send_rows(0, c))
    for load in loads[1:]:
        load.wait()

    def coefficients(c):
        at = raw_cols(c)
        for k in range(sections):
            a = ca[k, :, at] + SHIFT
            c_ = cc[k, :, at] + SHIFT
            b = cb[k, :, at]
            inverse = 1.0 / (a * c_ - b * b)
            ca[k, :, at] = a * inverse
            cc[k, :, at] = c_ * inverse
            cb[k, :, at] = b * inverse
    over(CHUNKS, coefficients)

    if detour:
        over(AHEAD, pass_on)

    top = lax.broadcasted_iota(jnp.int32, (height, cw), 0) == 0
    bottom = lax.broadcasted_iota(jnp.int32, (height, cw), 0) == height - 1

    def step(i):
        t, c = lax.div(i, CHUNKS), lax.rem(i, CHUNKS)
        if detour:
            @pl.when(i + AHEAD < SWEEPS * CHUNKS)
            def _():
                pass_on(i + AHEAD)
        for d, exists in ((0, has_up), (1, has_down)):
            @pl.when(exists)
            def _():
                row_copy(t, c, d).wait_recv()
        await_sections(t, c)
        at = raw_cols(c)
        for k in range(sections):
            r = []
            for comp in range(2):
                wide = u[t, comp, 2 + k, :, pl.ds(pl.multiple_of(c * cw, 128), cw + 2 * PAD)]
                mid = wide[:, PAD:PAD + cw]
                row = comp * sections + k
                above = jnp.where(top, row_in[t, 0, row:row + 1, at], pltpu.roll(mid, 1, 0))
                below = jnp.where(bottom, row_in[t, 1, row:row + 1, at], pltpu.roll(mid, height - 1, 0))
                before = pltpu.roll(wide, 1, 1)[:, PAD:PAD + cw]
                after = pltpu.roll(wide, cw + 2 * PAD - 1, 1)[:, PAD:PAD + cw]
                near = u[t, comp, 1 + k, :, cols(c)] + u[t, comp, 3 + k, :, cols(c)]
                far = u[t, comp, k, :, cols(c)] + u[t, comp, 4 + k, :, cols(c)]
                plane = (above + below) + (before + after)
                r.append((NEAR * near + FAR * far) + (PLANE * plane - g[comp, k, :, at]))
            b = cb[k, :, at]
            u[t + 1, 0, 2 + k, :, cols(c)] = cc[k, :, at] * r[0] - b * r[1]
            u[t + 1, 1, 2 + k, :, cols(c)] = ca[k, :, at] * r[1] - b * r[0]

        @pl.when(t < SWEEPS - 1)
        def _():
            each_section_copy(t + 1, c, start)
            send_rows(t + 1, c)

    over(SWEEPS * CHUNKS, step)

    store = pltpu.make_async_copy(u.at[SWEEPS, :, 2:sections + 2, :, PAD:PAD + width], out, out_sem)
    store.start()

    def drain(i):
        t, c = lax.div(i, CHUNKS), lax.rem(i, CHUNKS)
        each_section_copy(t, c, finish)
        for d, exists in ((0, has_down), (1, has_up)):
            @pl.when(exists)
            def _():
                row_copy(t, c, d).wait_send()
        if detour:
            for d, who in ((0, is_last), (1, is_first)):
                @pl.when(who)
                def _():
                    onward_copy(t, c, d).wait_send()
    over(SWEEPS * CHUNKS, drain)
    store.wait()


def on_device(n_stack, n_rows, field, hess_xx, hess_yy, hess_xy, gradient):
    sections, height, width = hess_xx.shape
    detour = n_stack == 8
    f32 = jnp.float32
    dma = pltpu.SemaphoreType.DMA
    return pl.pallas_call(
        functools.partial(kernel, n_stack, n_rows, detour),
        out_shape=jax.ShapeDtypeStruct(field.shape, f32),
        in_specs=[pl.BlockSpec(memory_space=pl.ANY)] * 5,
        out_specs=pl.BlockSpec(memory_space=pl.ANY),
        scratch_shapes=[
            pltpu.VMEM((SWEEPS + 1, 2, sections + 4, height, width + 2 * PAD), f32),
            pltpu.VMEM((2, sections, height, width), f32),
            pltpu.VMEM((sections, height, width), f32),
            pltpu.VMEM((sections, height, width), f32),
            pltpu.VMEM((sections, height, width), f32),
            pltpu.VMEM((SWEEPS, 2, 2 * sections, width), f32),
            pltpu.VMEM((SWEEPS, 2, 2 * sections, width), f32),
            pltpu.VMEM((SWEEPS, 2, 2, height // 2, width), f32),
            dma((5,)),
            dma((SWEEPS, CHUNKS, 4)),
            dma((SWEEPS, CHUNKS, 4)),
            dma((SWEEPS, CHUNKS)),
            dma((SWEEPS, CHUNKS)),
            dma((SWEEPS, CHUNKS)),
            dma((SWEEPS, CHUNKS)),
            dma(()),
        ],
        compiler_params=pltpu.CompilerParams(
            collective_id=0, has_side_effects=True, vmem_limit_bytes=40 * 1024 * 1024
        ),
        cost_estimate=pl.CostEstimate(
            flops=40 * SWEEPS * field.size, bytes_accessed=18 * field.size, transcendentals=0
        ),
    )(field, hess_xx, hess_yy, hess_xy, gradient)


def solution(mesh):
    cells = P("stack", "rows", None)
    fields = P(None, "stack", "rows", None)
    return jax.shard_map(
        functools.partial(on_device, mesh.shape["stack"], mesh.shape["rows"]),
        mesh=mesh, in_specs=(fields, cells, cells, cells, fields), out_specs=fields, check_vma=False,
    )
```

```python
import functools

import jax
import jax.numpy as jnp
from jax import lax
from jax.experimental import pallas as pl
from jax.experimental.pallas import tpu as pltpu
from jax.sharding import PartitionSpec as P

SWEEPS = 6
NEAR, FAR, PLANE, SHIFT = 1.0, 0.5, 1.0, 7.0
PAD = 128
CHUNKS = 4
AHEAD = 2


def kernel(n_stack, n_rows, detour, field, hxx, hyy, hxy, grad, out,
           u, g, ca, cc, cb, row_out, row_in, passing,
           load_sem, send_sem, recv_sem, pass_send, pass_in, pass_out, pass_recv, out_sem):
    sections, height, width = hxx.shape
    cw = width // CHUNKS
    half = height // 2
    s = lax.axis_index("stack")
    z = lax.axis_index("rows")
    has_left, has_right = s > 0, s < n_stack - 1
    has_up, has_down = z > 0, z < n_rows - 1
    left, right = (s - 1, z), (s + 1, z)
    up, down = (s, z - 1), (s, z + 1)
    sides = ((has_left, left), (has_right, right), (has_up, up), (has_down, down))

    lo, hi = n_stack // 2 - 1, n_stack // 2
    is_lo, is_hi, is_first, is_last = s == lo, s == hi, s == 0, s == n_stack - 1
    via_last, via_first = (n_stack - 1, z), (0, z)

    barrier = pltpu.get_barrier_semaphore()
    expected = jnp.int32(0)
    for exists, where in sides:
        expected = expected + exists.astype(jnp.int32)

        @pl.when(exists)
        def _():
            pl.semaphore_signal(barrier, inc=1, device_id=where)
    if detour:
        for who, peers in ((is_lo, (0, n_stack - 1)), (is_hi, (0, n_stack - 1)),
                           (is_first, (lo, hi)), (is_last, (lo, hi))):
            expected = expected + 2 * who.astype(jnp.int32)

            @pl.when(who)
            def _():
                for peer in peers:
                    pl.semaphore_signal(barrier, inc=1, device_id=(peer, z))

    loads = [
        pltpu.make_async_copy(field, u.at[0, :, 2:sections + 2, :, PAD:PAD + width], load_sem.at[0]),
        pltpu.make_async_copy(hxx, ca, load_sem.at[1]),
        pltpu.make_async_copy(hyy, cc, load_sem.at[2]),
        pltpu.make_async_copy(hxy, cb, load_sem.at[3]),
        pltpu.make_async_copy(grad, g, load_sem.at[4]),
    ]
    for load in loads:
        load.start()
    pl.semaphore_wait(barrier, expected)

    def cols(c):
        return pl.ds(pl.multiple_of(c * cw + PAD, 128), cw)

    def raw_cols(c):
        return pl.ds(pl.multiple_of(c * cw, 128), cw)

    def section_copy(t, c, d, rows, first=False):
        dst = u.at[t, :, 0:2, rows, cols(c)] if d == 0 else u.at[t, :, sections + 2:sections + 4, rows, cols(c)]
        if first:
            src = field.at[:, sections - 2:sections, rows, raw_cols(c)] if d == 0 else field.at[:, 0:2, rows, raw_cols(c)]
        else:
            src = u.at[t, :, sections:sections + 2, rows, cols(c)] if d == 0 else u.at[t, :, 2:4, rows, cols(c)]
        return pltpu.make_async_remote_copy(
            src_ref=src, dst_ref=dst, send_sem=send_sem.at[t, c, d], recv_sem=recv_sem.at[t, c, d],
            device_id=right if d == 0 else left)

    def pass_copy(t, c, d, first=False):
        rows = slice(half, height)
        if first:
            src = field.at[:, sections - 2:sections, rows, raw_cols(c)] if d == 0 else field.at[:, 0:2, rows, raw_cols(c)]
        else:
            src = u.at[t, :, sections:sections + 2, rows, cols(c)] if d == 0 else u.at[t, :, 2:4, rows, cols(c)]
        return pltpu.make_async_remote_copy(
            src_ref=src, dst_ref=passing.at[t, :, :, :, raw_cols(c)], send_sem=pass_send.at[t, c],
            recv_sem=pass_in.at[t, c], device_id=via_last if d == 0 else via_first)

    def onward_copy(t, c, d):
        rows = slice(half, height)
        dst = u.at[t, :, 0:2, rows, cols(c)] if d == 0 else u.at[t, :, sections + 2:sections + 4, rows, cols(c)]
        return pltpu.make_async_remote_copy(
            src_ref=passing.at[t, :, :, :, raw_cols(c)], dst_ref=dst, send_sem=pass_out.at[t, c],
            recv_sem=pass_recv.at[t, c], device_id=(hi if d == 0 else lo, z))

    def row_copy(t, c, d):
        return pltpu.make_async_remote_copy(
            src_ref=row_out.at[t, d, :, raw_cols(c)], dst_ref=row_in.at[t, d, :, raw_cols(c)],
            send_sem=send_sem.at[t, c, 2 + d], recv_sem=recv_sem.at[t, c, 2 + d],
            device_id=down if d == 0 else up)

    def each_section_copy(t, c, do, first=False):
        every, upper = slice(0, height), slice(0, half)
        for d, exists, split in ((0, has_right, is_lo), (1, has_left, is_hi)):
            if detour:
                @pl.when(split)
                def _():
                    do(section_copy(t, c, d, upper, first), pass_copy(t, c, d, first))

                @pl.when(exists & jnp.logical_not(split))
                def _():
                    do(section_copy(t, c, d, every, first), None)
            else:
                @pl.when(exists)
                def _():
                    do(section_copy(t, c, d, every, first), None)

    def start(copy, other):
        if other is not None:
            other.start()
        copy.start()

    def finish(copy, other):
        copy.wait_send()
        if other is not None:
            other.wait_send()

    def await_sections(t, c):
        every, upper = slice(0, height), slice(0, half)
        for d, exists, split in ((0, has_left, is_hi), (1, has_right, is_lo)):
            if detour:
                @pl.when(split)
                def _():
                    section_copy(t, c, d, upper).wait_recv()
                    onward_copy(t, c, d).wait_recv()

                @pl.when(exists & jnp.logical_not(split))
                def _():
                    section_copy(t, c, d, every).wait_recv()
            else:
                @pl.when(exists)
                def _():
                    section_copy(t, c, d, every).wait_recv()

    def send_rows(t, c):
        for d, exists, edge in ((0, has_down, height - 1), (1, has_up, 0)):
            for i in range(2):
                for k in range(sections):
                    at = i * sections + k
                    row_out[t, d, at:at + 1, raw_cols(c)] = u[t, i, 2 + k, edge:edge + 1, cols(c)]

            @pl.when(exists)
            def _():
                row_copy(t, c, d).start()

    def pass_on(j):
        t, c = lax.div(j, CHUNKS), lax.rem(j, CHUNKS)
        for d, who in ((0, is_last), (1, is_first)):
            @pl.when(who)
            def _():
                pass_copy(t, c, d).wait_recv()
                onward_copy(t, c, d).start()

    def over(count, body):
        lax.fori_loop(0, count, lambda i, _: (body(i), None)[1], None)

    over(CHUNKS, lambda c: each_section_copy(0, c, start, True))

    for t in range(SWEEPS):
        for at in (0, PAD + width):
            u[t, :, 2:sections + 2, :, at:at + PAD] = jnp.zeros((2, sections, height, PAD), jnp.float32)
    def zero(t):
        for exists, at in ((has_left, 0), (has_right, sections + 2)):
            @pl.when(jnp.logical_not(exists))
            def _():
                u[t, :, at:at + 2, :, PAD:PAD + width] = jnp.zeros((2, 2, height, width), jnp.float32)
        for d, exists in ((0, has_up), (1, has_down)):
            @pl.when(jnp.logical_not(exists))
            def _():
                row_in[t, d] = jnp.zeros((2 * sections, width), jnp.float32)
    over(SWEEPS, zero)

    loads[0].wait()
    over(CHUNKS, lambda c: send_rows(0, c))
    for load in loads[1:]:
        load.wait()

    def coefficients(c):
        at = raw_cols(c)
        for k in range(sections):
            a = ca[k, :, at] + SHIFT
            c_ = cc[k, :, at] + SHIFT
            b = cb[k, :, at]
            inverse = 1.0 / (a * c_ - b * b)
            ca[k, :, at] = a * inverse
            cc[k, :, at] = c_ * inverse
            cb[k, :, at] = b * inverse
    over(CHUNKS, coefficients)

    if detour:
        over(AHEAD, pass_on)

    def store(c):
        return pltpu.make_async_copy(
            u.at[SWEEPS, :, 2:sections + 2, :, cols(c)], out.at[:, :, :, raw_cols(c)], out_sem.at[c])

    top = lax.broadcasted_iota(jnp.int32, (height, cw), 0) == 0
    bottom = lax.broadcasted_iota(jnp.int32, (height, cw), 0) == height - 1

    def step(i):
        t, c = lax.div(i, CHUNKS), lax.rem(i, CHUNKS)
        if detour:
            @pl.when(i + AHEAD < SWEEPS * CHUNKS)
            def _():
                pass_on(i + AHEAD)
        for d, exists in ((0, has_up), (1, has_down)):
            @pl.when(exists)
            def _():
                row_copy(t, c, d).wait_recv()
        await_sections(t, c)
        at = raw_cols(c)
        for k in range(sections):
            r = []
            for comp in range(2):
                wide = u[t, comp, 2 + k, :, pl.ds(pl.multiple_of(c * cw, 128), cw + 2 * PAD)]
                mid = wide[:, PAD:PAD + cw]
                row = comp * sections + k
                above = jnp.where(top, row_in[t, 0, row:row + 1, at], pltpu.roll(mid, 1, 0))
                below = jnp.where(bottom, row_in[t, 1, row:row + 1, at], pltpu.roll(mid, height - 1, 0))
                before = pltpu.roll(wide, 1, 1)[:, PAD:PAD + cw]
                after = pltpu.roll(wide, cw + 2 * PAD - 1, 1)[:, PAD:PAD + cw]
                near = u[t, comp, 1 + k, :, cols(c)] + u[t, comp, 3 + k, :, cols(c)]
                far = u[t, comp, k, :, cols(c)] + u[t, comp, 4 + k, :, cols(c)]
                plane = (above + below) + (before + after)
                r.append((NEAR * near + FAR * far) + (PLANE * plane - g[comp, k, :, at]))
            b = cb[k, :, at]
            u[t + 1, 0, 2 + k, :, cols(c)] = cc[k, :, at] * r[0] - b * r[1]
            u[t + 1, 1, 2 + k, :, cols(c)] = ca[k, :, at] * r[1] - b * r[0]

        @pl.when(t < SWEEPS - 1)
        def _():
            each_section_copy(t + 1, c, start)
            send_rows(t + 1, c)

        @pl.when(t == SWEEPS - 1)
        def _():
            store(c).start()

    over(SWEEPS * CHUNKS, step)

    def drain(i):
        t, c = lax.div(i, CHUNKS), lax.rem(i, CHUNKS)
        each_section_copy(t, c, finish)
        for d, exists in ((0, has_down), (1, has_up)):
            @pl.when(exists)
            def _():
                row_copy(t, c, d).wait_send()
        if detour:
            for d, who in ((0, is_last), (1, is_first)):
                @pl.when(who)
                def _():
                    onward_copy(t, c, d).wait_send()
    over(SWEEPS * CHUNKS, drain)
    over(CHUNKS, lambda c: store(c).wait())


def on_device(n_stack, n_rows, field, hess_xx, hess_yy, hess_xy, gradient):
    sections, height, width = hess_xx.shape
    detour = n_stack == 8
    f32 = jnp.float32
    dma = pltpu.SemaphoreType.DMA
    return pl.pallas_call(
        functools.partial(kernel, n_stack, n_rows, detour),
        out_shape=jax.ShapeDtypeStruct(field.shape, f32),
        in_specs=[pl.BlockSpec(memory_space=pl.ANY)] * 5,
        out_specs=pl.BlockSpec(memory_space=pl.ANY),
        scratch_shapes=[
            pltpu.VMEM((SWEEPS + 1, 2, sections + 4, height, width + 2 * PAD), f32),
            pltpu.VMEM((2, sections, height, width), f32),
            pltpu.VMEM((sections, height, width), f32),
            pltpu.VMEM((sections, height, width), f32),
            pltpu.VMEM((sections, height, width), f32),
            pltpu.VMEM((SWEEPS, 2, 2 * sections, width), f32),
            pltpu.VMEM((SWEEPS, 2, 2 * sections, width), f32),
            pltpu.VMEM((SWEEPS, 2, 2, height // 2, width), f32),
            dma((5,)),
            dma((SWEEPS, CHUNKS, 4)),
            dma((SWEEPS, CHUNKS, 4)),
            dma((SWEEPS, CHUNKS)),
            dma((SWEEPS, CHUNKS)),
            dma((SWEEPS, CHUNKS)),
            dma((SWEEPS, CHUNKS)),
            dma((CHUNKS,)),
        ],
        compiler_params=pltpu.CompilerParams(
            collective_id=0, has_side_effects=True, vmem_limit_bytes=60 * 1024 * 1024
        ),
        cost_estimate=pl.CostEstimate(
            flops=40 * SWEEPS * field.size, bytes_accessed=18 * field.size, transcendentals=0
        ),
    )(field, hess_xx, hess_yy, hess_xy, gradient)


def solution(mesh):
    cells = P("stack", "rows", None)
    fields = P(None, "stack", "rows", None)
    return jax.shard_map(
        functools.partial(on_device, mesh.shape["stack"], mesh.shape["rows"]),
        mesh=mesh, in_specs=(fields, cells, cells, cells, fields), out_specs=fields, check_vma=False,
    )
```

```python
import functools

import jax
import jax.numpy as jnp
from jax import lax
from jax.experimental import pallas as pl
from jax.experimental.pallas import tpu as pltpu
from jax.sharding import PartitionSpec as P

SWEEPS = 6
NEAR, FAR, PLANE, SHIFT = 1.0, 0.5, 1.0, 7.0
PAD = 128
CHUNKS = 4
AHEAD = 1


def kernel(n_stack, n_rows, detour, field, hxx, hyy, hxy, grad, out,
           u, g, ca, cc, cb, row_out, row_in, passing,
           load_sem, send_sem, recv_sem, pass_send, pass_in, pass_out, pass_recv, out_sem):
    sections, height, width = hxx.shape
    cw = width // CHUNKS
    half = height // 2
    s = lax.axis_index("stack")
    z = lax.axis_index("rows")
    has_left, has_right = s > 0, s < n_stack - 1
    has_up, has_down = z > 0, z < n_rows - 1
    left, right = (s - 1, z), (s + 1, z)
    up, down = (s, z - 1), (s, z + 1)
    sides = ((has_left, left), (has_right, right), (has_up, up), (has_down, down))

    lo, hi = n_stack // 2 - 1, n_stack // 2
    is_lo, is_hi, is_first, is_last = s == lo, s == hi, s == 0, s == n_stack - 1
    via_last, via_first = (n_stack - 1, z), (0, z)

    barrier = pltpu.get_barrier_semaphore()
    expected = jnp.int32(0)
    for exists, where in sides:
        expected = expected + exists.astype(jnp.int32)

        @pl.when(exists)
        def _():
            pl.semaphore_signal(barrier, inc=1, device_id=where)
    if detour:
        for who, peers in ((is_lo, (0, n_stack - 1)), (is_hi, (0, n_stack - 1)),
                           (is_first, (lo, hi)), (is_last, (lo, hi))):
            expected = expected + 2 * who.astype(jnp.int32)

            @pl.when(who)
            def _():
                for peer in peers:
                    pl.semaphore_signal(barrier, inc=1, device_id=(peer, z))

    loads = [
        pltpu.make_async_copy(field, u.at[0, :, 2:sections + 2, :, PAD:PAD + width], load_sem.at[0]),
        pltpu.make_async_copy(hxx, ca, load_sem.at[1]),
        pltpu.make_async_copy(hyy, cc, load_sem.at[2]),
        pltpu.make_async_copy(hxy, cb, load_sem.at[3]),
        pltpu.make_async_copy(grad, g, load_sem.at[4]),
    ]
    for load in loads:
        load.start()
    pl.semaphore_wait(barrier, expected)

    def cols(c):
        return pl.ds(pl.multiple_of(c * cw + PAD, 128), cw)

    def raw_cols(c):
        return pl.ds(pl.multiple_of(c * cw, 128), cw)

    def section_copy(t, c, d, rows, first=False):
        dst = u.at[t, :, 0:2, rows, cols(c)] if d == 0 else u.at[t, :, sections + 2:sections + 4, rows, cols(c)]
        if first:
            src = field.at[:, sections - 2:sections, rows, raw_cols(c)] if d == 0 else field.at[:, 0:2, rows, raw_cols(c)]
        else:
            src = u.at[t, :, sections:sections + 2, rows, cols(c)] if d == 0 else u.at[t, :, 2:4, rows, cols(c)]
        return pltpu.make_async_remote_copy(
            src_ref=src, dst_ref=dst, send_sem=send_sem.at[t, c, d], recv_sem=recv_sem.at[t, c, d],
            device_id=right if d == 0 else left)

    def pass_copy(t, c, d, first=False):
        rows = slice(half, height)
        if first:
            src = field.at[:, sections - 2:sections, rows, raw_cols(c)] if d == 0 else field.at[:, 0:2, rows, raw_cols(c)]
        else:
            src = u.at[t, :, sections:sections + 2, rows, cols(c)] if d == 0 else u.at[t, :, 2:4, rows, cols(c)]
        return pltpu.make_async_remote_copy(
            src_ref=src, dst_ref=passing.at[t, :, :, :, raw_cols(c)], send_sem=pass_send.at[t, c],
            recv_sem=pass_in.at[t, c], device_id=via_last if d == 0 else via_first)

    def onward_copy(t, c, d):
        rows = slice(half, height)
        dst = u.at[t, :, 0:2, rows, cols(c)] if d == 0 else u.at[t, :, sections + 2:sections + 4, rows, cols(c)]
        return pltpu.make_async_remote_copy(
            src_ref=passing.at[t, :, :, :, raw_cols(c)], dst_ref=dst, send_sem=pass_out.at[t, c],
            recv_sem=pass_recv.at[t, c], device_id=(hi if d == 0 else lo, z))

    def row_copy(t, c, d):
        return pltpu.make_async_remote_copy(
            src_ref=row_out.at[t, d, :, raw_cols(c)], dst_ref=row_in.at[t, d, :, raw_cols(c)],
            send_sem=send_sem.at[t, c, 2 + d], recv_sem=recv_sem.at[t, c, 2 + d],
            device_id=down if d == 0 else up)

    def each_section_copy(t, c, do, first=False, only=(0, 1)):
        every, upper = slice(0, height), slice(0, half)
        for d, exists, split in ((0, has_right, is_lo), (1, has_left, is_hi)):
            if d not in only:
                continue
            if detour:
                @pl.when(split)
                def _():
                    do(section_copy(t, c, d, upper, first), pass_copy(t, c, d, first))

                @pl.when(exists & jnp.logical_not(split))
                def _():
                    do(section_copy(t, c, d, every, first), None)
            else:
                @pl.when(exists)
                def _():
                    do(section_copy(t, c, d, every, first), None)

    def start(copy, other):
        if other is not None:
            other.start()
        copy.start()

    def finish(copy, other):
        copy.wait_send()
        if other is not None:
            other.wait_send()

    def await_sections(t, c):
        every, upper = slice(0, height), slice(0, half)
        for d, exists, split in ((0, has_left, is_hi), (1, has_right, is_lo)):
            if detour:
                @pl.when(split)
                def _():
                    section_copy(t, c, d, upper).wait_recv()
                    onward_copy(t, c, d).wait_recv()

                @pl.when(exists & jnp.logical_not(split))
                def _():
                    section_copy(t, c, d, every).wait_recv()
            else:
                @pl.when(exists)
                def _():
                    section_copy(t, c, d, every).wait_recv()

    def send_rows(t, c):
        for d, exists, edge in ((0, has_down, height - 1), (1, has_up, 0)):
            for i in range(2):
                for k in range(sections):
                    at = i * sections + k
                    row_out[t, d, at:at + 1, raw_cols(c)] = u[t, i, 2 + k, edge:edge + 1, cols(c)]

            @pl.when(exists)
            def _():
                row_copy(t, c, d).start()

    def pass_on(j):
        t, c = lax.div(j, CHUNKS), lax.rem(j, CHUNKS)
        for d, who in ((0, is_last), (1, is_first)):
            @pl.when(who)
            def _():
                pass_copy(t, c, d).wait_recv()
                onward_copy(t, c, d).start()

    def over(count, body):
        lax.fori_loop(0, count, lambda i, _: (body(i), None)[1], None)

    over(CHUNKS, lambda c: each_section_copy(0, c, start, True))

    for t in range(SWEEPS):
        for at in (0, PAD + width):
            u[t, :, 2:sections + 2, :, at:at + PAD] = jnp.zeros((2, sections, height, PAD), jnp.float32)
    def zero(t):
        for exists, at in ((has_left, 0), (has_right, sections + 2)):
            @pl.when(jnp.logical_not(exists))
            def _():
                u[t, :, at:at + 2, :, PAD:PAD + width] = jnp.zeros((2, 2, height, width), jnp.float32)
        for d, exists in ((0, has_up), (1, has_down)):
            @pl.when(jnp.logical_not(exists))
            def _():
                row_in[t, d] = jnp.zeros((2 * sections, width), jnp.float32)
    over(SWEEPS, zero)

    loads[0].wait()
    over(CHUNKS, lambda c: send_rows(0, c))
    for load in loads[1:]:
        load.wait()

    def coefficients(c):
        at = raw_cols(c)
        for k in range(sections):
            a = ca[k, :, at] + SHIFT
            c_ = cc[k, :, at] + SHIFT
            b = cb[k, :, at]
            inverse = 1.0 / (a * c_ - b * b)
            ca[k, :, at] = a * inverse
            cc[k, :, at] = c_ * inverse
            cb[k, :, at] = b * inverse
    over(CHUNKS, coefficients)

    if detour:
        over(AHEAD, pass_on)

    def store(c):
        return pltpu.make_async_copy(
            u.at[SWEEPS, :, 2:sections + 2, :, cols(c)], out.at[:, :, :, raw_cols(c)], out_sem.at[c])

    top = lax.broadcasted_iota(jnp.int32, (height, cw), 0) == 0
    bottom = lax.broadcasted_iota(jnp.int32, (height, cw), 0) == height - 1

    def step(i):
        t, c = lax.div(i, CHUNKS), lax.rem(i, CHUNKS)
        if detour:
            @pl.when(i + AHEAD < SWEEPS * CHUNKS)
            def _():
                pass_on(i + AHEAD)
        for d, exists in ((0, has_up), (1, has_down)):
            @pl.when(exists)
            def _():
                row_copy(t, c, d).wait_recv()
        await_sections(t, c)
        at = raw_cols(c)
        for k in range(sections):
            r = []
            for comp in range(2):
                wide = u[t, comp, 2 + k, :, pl.ds(pl.multiple_of(c * cw, 128), cw + 2 * PAD)]
                mid = wide[:, PAD:PAD + cw]
                row = comp * sections + k
                above = jnp.where(top, row_in[t, 0, row:row + 1, at], pltpu.roll(mid, 1, 0))
                below = jnp.where(bottom, row_in[t, 1, row:row + 1, at], pltpu.roll(mid, height - 1, 0))
                before = pltpu.roll(wide, 1, 1)[:, PAD:PAD + cw]
                after = pltpu.roll(wide, cw + 2 * PAD - 1, 1)[:, PAD:PAD + cw]
                near = u[t, comp, 1 + k, :, cols(c)] + u[t, comp, 3 + k, :, cols(c)]
                far = u[t, comp, k, :, cols(c)] + u[t, comp, 4 + k, :, cols(c)]
                plane = (above + below) + (before + after)
                r.append((NEAR * near + FAR * far) + (PLANE * plane - g[comp, k, :, at]))
            b = cb[k, :, at]
            u[t + 1, 0, 2 + k, :, cols(c)] = cc[k, :, at] * r[0] - b * r[1]
            u[t + 1, 1, 2 + k, :, cols(c)] = ca[k, :, at] * r[1] - b * r[0]
            if k == 1 or k == sections - 1:
                @pl.when(t < SWEEPS - 1)
                def _():
                    each_section_copy(t + 1, c, start, only=(1,) if k == 1 else (0,))

        @pl.when(t < SWEEPS - 1)
        def _():
            send_rows(t + 1, c)

        @pl.when(t == SWEEPS - 1)
        def _():
            store(c).start()

    over(SWEEPS * CHUNKS, step)

    def drain(i):
        t, c = lax.div(i, CHUNKS), lax.rem(i, CHUNKS)
        each_section_copy(t, c, finish)
        for d, exists in ((0, has_down), (1, has_up)):
            @pl.when(exists)
            def _():
                row_copy(t, c, d).wait_send()
        if detour:
            for d, who in ((0, is_last), (1, is_first)):
                @pl.when(who)
                def _():
                    onward_copy(t, c, d).wait_send()
    over(SWEEPS * CHUNKS, drain)
    over(CHUNKS, lambda c: store(c).wait())


def on_device(n_stack, n_rows, field, hess_xx, hess_yy, hess_xy, gradient):
    sections, height, width = hess_xx.shape
    detour = n_stack == 8
    f32 = jnp.float32
    dma = pltpu.SemaphoreType.DMA
    return pl.pallas_call(
        functools.partial(kernel, n_stack, n_rows, detour),
        out_shape=jax.ShapeDtypeStruct(field.shape, f32),
        in_specs=[pl.BlockSpec(memory_space=pl.ANY)] * 5,
        out_specs=pl.BlockSpec(memory_space=pl.ANY),
        scratch_shapes=[
            pltpu.VMEM((SWEEPS + 1, 2, sections + 4, height, width + 2 * PAD), f32),
            pltpu.VMEM((2, sections, height, width), f32),
            pltpu.VMEM((sections, height, width), f32),
            pltpu.VMEM((sections, height, width), f32),
            pltpu.VMEM((sections, height, width), f32),
            pltpu.VMEM((SWEEPS, 2, 2 * sections, width), f32),
            pltpu.VMEM((SWEEPS, 2, 2 * sections, width), f32),
            pltpu.VMEM((SWEEPS, 2, 2, height // 2, width), f32),
            dma((5,)),
            dma((SWEEPS, CHUNKS, 4)),
            dma((SWEEPS, CHUNKS, 4)),
            dma((SWEEPS, CHUNKS)),
            dma((SWEEPS, CHUNKS)),
            dma((SWEEPS, CHUNKS)),
            dma((SWEEPS, CHUNKS)),
            dma((CHUNKS,)),
        ],
        compiler_params=pltpu.CompilerParams(
            collective_id=0, has_side_effects=True, vmem_limit_bytes=60 * 1024 * 1024
        ),
        cost_estimate=pl.CostEstimate(
            flops=40 * SWEEPS * field.size, bytes_accessed=18 * field.size, transcendentals=0
        ),
    )(field, hess_xx, hess_yy, hess_xy, gradient)


def solution(mesh):
    cells = P("stack", "rows", None)
    fields = P(None, "stack", "rows", None)
    return jax.shard_map(
        functools.partial(on_device, mesh.shape["stack"], mesh.shape["rows"]),
        mesh=mesh, in_specs=(fields, cells, cells, cells, fields), out_specs=fields, check_vma=False,
    )
```

```python
import functools

import jax
import jax.numpy as jnp
from jax import lax
from jax.experimental import pallas as pl
from jax.experimental.pallas import tpu as pltpu
from jax.sharding import PartitionSpec as P

SWEEPS = 6
NEAR, FAR, PLANE, SHIFT = 1.0, 0.5, 1.0, 7.0
PAD = 128
CHUNKS = 4
AHEAD = 1


def kernel(n_stack, n_rows, detour, field, hxx, hyy, hxy, grad, out,
           u, g, ca, cc, cb, row_out, row_in, passing,
           load_sem, send_sem, recv_sem, pass_send, pass_in, pass_out, pass_recv, out_sem):
    sections, height, width = hxx.shape
    cw = width // CHUNKS
    half = height // 2
    s = lax.axis_index("stack")
    z = lax.axis_index("rows")
    has_left, has_right = s > 0, s < n_stack - 1
    has_up, has_down = z > 0, z < n_rows - 1
    left, right = (s - 1, z), (s + 1, z)
    up, down = (s, z - 1), (s, z + 1)
    sides = ((has_left, left), (has_right, right), (has_up, up), (has_down, down))

    lo, hi = n_stack // 2 - 1, n_stack // 2
    is_lo, is_hi, is_first, is_last = s == lo, s == hi, s == 0, s == n_stack - 1
    via_last, via_first = (n_stack - 1, z), (0, z)

    barrier = pltpu.get_barrier_semaphore()
    expected = jnp.int32(0)
    for exists, where in sides:
        expected = expected + exists.astype(jnp.int32)

        @pl.when(exists)
        def _():
            pl.semaphore_signal(barrier, inc=1, device_id=where)
    if detour:
        for who, peers in ((is_lo, (0, n_stack - 1)), (is_hi, (0, n_stack - 1)),
                           (is_first, (lo, hi)), (is_last, (lo, hi))):
            expected = expected + 2 * who.astype(jnp.int32)

            @pl.when(who)
            def _():
                for peer in peers:
                    pl.semaphore_signal(barrier, inc=1, device_id=(peer, z))

    loads = [
        pltpu.make_async_copy(field, u.at[0, :, 2:sections + 2, :, PAD:PAD + width], load_sem.at[0]),
        pltpu.make_async_copy(hxx, ca, load_sem.at[1]),
        pltpu.make_async_copy(hyy, cc, load_sem.at[2]),
        pltpu.make_async_copy(hxy, cb, load_sem.at[3]),
        pltpu.make_async_copy(grad, g, load_sem.at[4]),
    ]
    for load in loads:
        load.start()
    pl.semaphore_wait(barrier, expected)

    def cols(c):
        return pl.ds(pl.multiple_of(c * cw + PAD, 128), cw)

    def raw_cols(c):
        return pl.ds(pl.multiple_of(c * cw, 128), cw)

    def section_copy(t, c, d, rows, first=False):
        dst = u.at[t, :, 0:2, rows, cols(c)] if d == 0 else u.at[t, :, sections + 2:sections + 4, rows, cols(c)]
        if first:
            src = field.at[:, sections - 2:sections, rows, raw_cols(c)] if d == 0 else field.at[:, 0:2, rows, raw_cols(c)]
        else:
            src = u.at[t, :, sections:sections + 2, rows, cols(c)] if d == 0 else u.at[t, :, 2:4, rows, cols(c)]
        return pltpu.make_async_remote_copy(
            src_ref=src, dst_ref=dst, send_sem=send_sem.at[t, c, d], recv_sem=recv_sem.at[t, c, d],
            device_id=right if d == 0 else left)

    def pass_copy(t, c, d, first=False):
        rows = slice(half, height)
        if first:
            src = field.at[:, sections - 2:sections, rows, raw_cols(c)] if d == 0 else field.at[:, 0:2, rows, raw_cols(c)]
        else:
            src = u.at[t, :, sections:sections + 2, rows, cols(c)] if d == 0 else u.at[t, :, 2:4, rows, cols(c)]
        return pltpu.make_async_remote_copy(
            src_ref=src, dst_ref=passing.at[t, :, :, :, raw_cols(c)], send_sem=pass_send.at[t, c],
            recv_sem=pass_in.at[t, c], device_id=via_last if d == 0 else via_first)

    def onward_copy(t, c, d):
        rows = slice(half, height)
        dst = u.at[t, :, 0:2, rows, cols(c)] if d == 0 else u.at[t, :, sections + 2:sections + 4, rows, cols(c)]
        return pltpu.make_async_remote_copy(
            src_ref=passing.at[t, :, :, :, raw_cols(c)], dst_ref=dst, send_sem=pass_out.at[t, c],
            recv_sem=pass_recv.at[t, c], device_id=(hi if d == 0 else lo, z))

    def row_copy(t, c, d):
        return pltpu.make_async_remote_copy(
            src_ref=row_out.at[t, d, :, raw_cols(c)], dst_ref=row_in.at[t, d, :, raw_cols(c)],
            send_sem=send_sem.at[t, c, 2 + d], recv_sem=recv_sem.at[t, c, 2 + d],
            device_id=down if d == 0 else up)

    def each_section_copy(t, c, do, first=False, only=(0, 1)):
        every, upper = slice(0, height), slice(0, half)
        for d, exists, split in ((0, has_right, is_lo), (1, has_left, is_hi)):
            if d not in only:
                continue
            if detour:
                @pl.when(split)
                def _():
                    do(section_copy(t, c, d, upper, first), pass_copy(t, c, d, first))

                @pl.when(exists & jnp.logical_not(split))
                def _():
                    do(section_copy(t, c, d, every, first), None)
            else:
                @pl.when(exists)
                def _():
                    do(section_copy(t, c, d, every, first), None)

    def start(copy, other):
        if other is not None:
            other.start()
        copy.start()

    def finish(copy, other):
        copy.wait_send()
        if other is not None:
            other.wait_send()

    def await_sections(t, c, only):
        every, upper = slice(0, height), slice(0, half)
        for d, exists, split in ((0, has_left, is_hi), (1, has_right, is_lo)):
            if d != only:
                continue
            if detour:
                @pl.when(split)
                def _():
                    section_copy(t, c, d, upper).wait_recv()
                    onward_copy(t, c, d).wait_recv()

                @pl.when(exists & jnp.logical_not(split))
                def _():
                    section_copy(t, c, d, every).wait_recv()
            else:
                @pl.when(exists)
                def _():
                    section_copy(t, c, d, every).wait_recv()

    def send_rows(t, c):
        for d, exists, edge in ((0, has_down, height - 1), (1, has_up, 0)):
            for i in range(2):
                for k in range(sections):
                    at = i * sections + k
                    row_out[t, d, at:at + 1, raw_cols(c)] = u[t, i, 2 + k, edge:edge + 1, cols(c)]

            @pl.when(exists)
            def _():
                row_copy(t, c, d).start()

    def pass_on(j):
        t, c = lax.div(j, CHUNKS), lax.rem(j, CHUNKS)
        for d, who in ((0, is_last), (1, is_first)):
            @pl.when(who)
            def _():
                pass_copy(t, c, d).wait_recv()
                onward_copy(t, c, d).start()

    def over(count, body):
        lax.fori_loop(0, count, lambda i, _: (body(i), None)[1], None)

    over(CHUNKS, lambda c: each_section_copy(0, c, start, True))

    for t in range(SWEEPS):
        for at in (0, PAD + width):
            u[t, :, 2:sections + 2, :, at:at + PAD] = jnp.zeros((2, sections, height, PAD), jnp.float32)
    def zero(t):
        for exists, at in ((has_left, 0), (has_right, sections + 2)):
            @pl.when(jnp.logical_not(exists))
            def _():
                u[t, :, at:at + 2, :, PAD:PAD + width] = jnp.zeros((2, 2, height, width), jnp.float32)
        for d, exists in ((0, has_up), (1, has_down)):
            @pl.when(jnp.logical_not(exists))
            def _():
                row_in[t, d] = jnp.zeros((2 * sections, width), jnp.float32)
    over(SWEEPS, zero)

    loads[0].wait()
    over(CHUNKS, lambda c: send_rows(0, c))
    for load in loads[1:]:
        load.wait()

    def coefficients(c):
        at = raw_cols(c)
        for k in range(sections):
            a = ca[k, :, at] + SHIFT
            c_ = cc[k, :, at] + SHIFT
            b = cb[k, :, at]
            inverse = 1.0 / (a * c_ - b * b)
            ca[k, :, at] = a * inverse
            cc[k, :, at] = c_ * inverse
            cb[k, :, at] = b * inverse
    over(CHUNKS, coefficients)

    if detour:
        over(AHEAD, pass_on)

    def store(c):
        return pltpu.make_async_copy(
            u.at[SWEEPS, :, 2:sections + 2, :, cols(c)], out.at[:, :, :, raw_cols(c)], out_sem.at[c])

    top = lax.broadcasted_iota(jnp.int32, (height, cw), 0) == 0
    bottom = lax.broadcasted_iota(jnp.int32, (height, cw), 0) == height - 1

    def step(i):
        t, c = lax.div(i, CHUNKS), lax.rem(i, CHUNKS)
        if detour:
            @pl.when(i + AHEAD < SWEEPS * CHUNKS)
            def _():
                pass_on(i + AHEAD)
        for d, exists in ((0, has_up), (1, has_down)):
            @pl.when(exists)
            def _():
                row_copy(t, c, d).wait_recv()
        at = raw_cols(c)
        for k in range(sections):
            if k == 0:
                await_sections(t, c, 0)
            if k == sections - 2:
                await_sections(t, c, 1)
            r = []
            for comp in range(2):
                wide = u[t, comp, 2 + k, :, pl.ds(pl.multiple_of(c * cw, 128), cw + 2 * PAD)]
                mid = wide[:, PAD:PAD + cw]
                row = comp * sections + k
                above = jnp.where(top, row_in[t, 0, row:row + 1, at], pltpu.roll(mid, 1, 0))
                below = jnp.where(bottom, row_in[t, 1, row:row + 1, at], pltpu.roll(mid, height - 1, 0))
                before = pltpu.roll(wide, 1, 1)[:, PAD:PAD + cw]
                after = pltpu.roll(wide, cw + 2 * PAD - 1, 1)[:, PAD:PAD + cw]
                near = u[t, comp, 1 + k, :, cols(c)] + u[t, comp, 3 + k, :, cols(c)]
                far = u[t, comp, k, :, cols(c)] + u[t, comp, 4 + k, :, cols(c)]
                plane = (above + below) + (before + after)
                r.append((NEAR * near + FAR * far) + (PLANE * plane - g[comp, k, :, at]))
            b = cb[k, :, at]
            u[t + 1, 0, 2 + k, :, cols(c)] = cc[k, :, at] * r[0] - b * r[1]
            u[t + 1, 1, 2 + k, :, cols(c)] = ca[k, :, at] * r[1] - b * r[0]
            if k == 1 or k == sections - 1:
                @pl.when(t < SWEEPS - 1)
                def _():
                    each_section_copy(t + 1, c, start, only=(1,) if k == 1 else (0,))

        @pl.when(t < SWEEPS - 1)
        def _():
            send_rows(t + 1, c)

        @pl.when(t == SWEEPS - 1)
        def _():
            store(c).start()

    over(SWEEPS * CHUNKS, step)

    def drain(i):
        t, c = lax.div(i, CHUNKS), lax.rem(i, CHUNKS)
        each_section_copy(t, c, finish)
        for d, exists in ((0, has_down), (1, has_up)):
            @pl.when(exists)
            def _():
                row_copy(t, c, d).wait_send()
        if detour:
            for d, who in ((0, is_last), (1, is_first)):
                @pl.when(who)
                def _():
                    onward_copy(t, c, d).wait_send()
    over(SWEEPS * CHUNKS, drain)
    over(CHUNKS, lambda c: store(c).wait())


def on_device(n_stack, n_rows, field, hess_xx, hess_yy, hess_xy, gradient):
    sections, height, width = hess_xx.shape
    detour = n_stack == 8
    f32 = jnp.float32
    dma = pltpu.SemaphoreType.DMA
    return pl.pallas_call(
        functools.partial(kernel, n_stack, n_rows, detour),
        out_shape=jax.ShapeDtypeStruct(field.shape, f32),
        in_specs=[pl.BlockSpec(memory_space=pl.ANY)] * 5,
        out_specs=pl.BlockSpec(memory_space=pl.ANY),
        scratch_shapes=[
            pltpu.VMEM((SWEEPS + 1, 2, sections + 4, height, width + 2 * PAD), f32),
            pltpu.VMEM((2, sections, height, width), f32),
            pltpu.VMEM((sections, height, width), f32),
            pltpu.VMEM((sections, height, width), f32),
            pltpu.VMEM((sections, height, width), f32),
            pltpu.VMEM((SWEEPS, 2, 2 * sections, width), f32),
            pltpu.VMEM((SWEEPS, 2, 2 * sections, width), f32),
            pltpu.VMEM((SWEEPS, 2, 2, height // 2, width), f32),
            dma((5,)),
            dma((SWEEPS, CHUNKS, 4)),
            dma((SWEEPS, CHUNKS, 4)),
            dma((SWEEPS, CHUNKS)),
            dma((SWEEPS, CHUNKS)),
            dma((SWEEPS, CHUNKS)),
            dma((SWEEPS, CHUNKS)),
            dma((CHUNKS,)),
        ],
        compiler_params=pltpu.CompilerParams(
            collective_id=0, has_side_effects=True, vmem_limit_bytes=60 * 1024 * 1024
        ),
        cost_estimate=pl.CostEstimate(
            flops=40 * SWEEPS * field.size, bytes_accessed=18 * field.size, transcendentals=0
        ),
    )(field, hess_xx, hess_yy, hess_xy, gradient)


def solution(mesh):
    cells = P("stack", "rows", None)
    fields = P(None, "stack", "rows", None)
    return jax.shard_map(
        functools.partial(on_device, mesh.shape["stack"], mesh.shape["rows"]),
        mesh=mesh, in_specs=(fields, cells, cells, cells, fields), out_specs=fields, check_vma=False,
    )
```
